512 devices in a mesh: tok: 4 (over x_lo, core), exp: 128 (over y, x_hi, z).
Axes of the slice: x: 4 (x_hi: 2, x_lo: 2; x = x_hi * 2 + x_lo), y: 4, z: 16, core: 2. Of those that a mesh axis runs over, the one named last changes fastest.
Arguments:
- tokens: bfloat16 [128, 1024, 1024], P('exp', 'tok'), may hold values from -6 to 6
- upstream: bfloat16 [128, 1024, 1024], P('exp', 'tok'), may hold values from -6 to 6
- dispatch: bfloat16 [128, 1024, 128], P('exp', 'tok'), may hold values from 0 to 1, as said below
- combine: bfloat16 [128, 1024, 128], P('exp', 'tok'), may hold values from 0 to 1, as said below
- w_in: bfloat16 [128, 1024, 2048], P('exp', None, 'tok'), may hold values from -0.1875 to 0.1875
- w_out: bfloat16 [128, 2048, 1024], P('exp', 'tok'), may hold values from -0.125 to 0.125
- slot_keys: bfloat16 [1024, 128], replicated, may hold values from -0.1875 to 0.1875
Outputs:
- token_grad: bfloat16 [128, 1024, 1024], P('exp', 'tok')
The draws below stay inside these ranges and needn't reach their ends.
Inputs may be any that keep to these rules, and one draw needn't show every extreme that they name: `dispatch`: for each image and slot the entries over the image's tokens are positive and sum to one up to rounding. `combine`: for each token the entries over the 128 slots are positive and sum to one up to rounding.
All inputs are finite; a program needn't handle non-finite values.
Results may differ from the reference program's by a relative error of at most 0.025.
Values may be sent and summed in bfloat16 or wider, within the bound.
No kernel may reach another device: no remote copies, remote signals or barrier semaphores. Data moves between devices by JAX's collectives and lax.ppermute only.
A program may use at most 64 MiB of HBM per device.

```python
import jax
import jax.numpy as jnp
from jax import lax

D = 1024
HID = 2048
PATCHES = 1024
EXPERTS = 128
IMAGES = 128
N_TOK = 4
N_EXP = 128


def draw_dispatch(key, part):
    logits = jax.random.normal(jax.random.fold_in(key, 11), (IMAGES, PATCHES, EXPERTS), jnp.float32)
    logits = 2.5 * logits
    return jax.nn.softmax(logits, axis=1).astype(jnp.bfloat16)


def draw_combine(key, part):
    logits = jax.random.normal(jax.random.fold_in(key, 21), (IMAGES, PATCHES, EXPERTS), jnp.float32)
    logits = 1.5 * logits
    return jax.nn.softmax(logits, axis=2).astype(jnp.bfloat16)


def steps_of(stream_key, dims, split, low, largest):
    def one(axis_at, blocks):
        heights = jax.random.uniform(jax.random.fold_in(jax.random.fold_in(stream_key, 6), axis_at), (blocks,), jnp.float32, low / len(split), largest / len(split))
        return jnp.repeat(jnp.exp(heights), dims[axis_at] // blocks).reshape((-1,) + (1,) * (len(dims) - axis_at - 1))

    level = one(*split[0])
    for cut in split[1:]:
        level = level * one(*cut)
    return level


def scatter_about(key, extent, spread, most, pieces=(), dtype=jnp.bfloat16):
    values = spread * jax.random.normal(key, extent, jnp.float32)
    if pieces:
        values = values * steps_of(key, extent, pieces, -0.22, 0.18)
    return jnp.clip(values, -most, most).astype(dtype)


def setup_inputs(seed: int = 0) -> dict:
    keys = jax.random.split(jax.random.key(seed), 8)
    tokens = scatter_about(keys[0], (IMAGES, PATCHES, D), 1.0, 6.0, ((0, 128), (1, 4)))
    upstream = scatter_about(keys[1], (IMAGES, PATCHES, D), 1.0, 6.0, ((0, 128), (1, 4)))
    dispatch = draw_dispatch(jax.random.fold_in(keys[7], 71), 0)
    combine = draw_combine(jax.random.fold_in(keys[7], 71), 0)
    w_in = scatter_about(keys[4], (EXPERTS, D, HID), D ** -0.5, 0.1875, ((0, 128), (2, 4)))
    w_out = scatter_about(keys[5], (EXPERTS, HID, D), HID ** -0.5, 0.125, ((0, 128), (1, 4)))
    slot_keys = scatter_about(keys[6], (D, EXPERTS), D ** -0.5, 0.1875)
    return dict(tokens=tokens, upstream=upstream, dispatch=dispatch, combine=combine, w_in=w_in, w_out=w_out, slot_keys=slot_keys)


def gelu_parts(pre_act):
    inside = 0.7978845608 * (pre_act + 0.044715 * pre_act * pre_act * pre_act)
    tanh_val = jnp.tanh(inside)
    gelu_value = 0.5 * pre_act * (1.0 + tanh_val)
    gelu_slope = 0.5 * (1.0 + tanh_val) + 0.5 * pre_act * (1.0 - tanh_val * tanh_val) * 0.7978845608 * (1.0 + 3.0 * 0.044715 * pre_act * pre_act)
    return gelu_value, gelu_slope


def group_total(partials):
    rounded = lax.optimization_barrier(partials.astype(jnp.bfloat16))
    return jnp.sum(rounded.astype(jnp.float32), axis=0).astype(jnp.bfloat16)


def reference(tokens, upstream, dispatch, combine, w_in, w_out, slot_keys):
    shard = PATCHES // N_TOK
    hidden_split = HID // N_TOK

    def token_forward(items):
        tok_image, grad_image, disp_image, comb_image = items
        tok_groups = tok_image.astype(jnp.float32).reshape(N_TOK, shard, D)
        grad_groups = grad_image.astype(jnp.float32).reshape(N_TOK, shard, D)
        disp_groups = disp_image.astype(jnp.float32).reshape(N_TOK, shard, N_EXP)
        comb_groups = comb_image.astype(jnp.float32).reshape(N_TOK, shard, N_EXP)
        slot_input = group_total(jnp.einsum("tms,tmd->tsd", disp_groups, tok_groups))
        slot_grad = group_total(jnp.einsum("tms,tmd->tsd", comb_groups, grad_groups))
        return slot_input, slot_grad

    slot_input, slot_grad = lax.map(token_forward, (tokens, upstream, dispatch, combine))

    def expert_step(items):
        input_rows, grad_rows, w_first, w_second = items
        first_groups = w_first.astype(jnp.float32).reshape(D, N_TOK, hidden_split)
        second_groups = w_second.astype(jnp.float32).reshape(N_TOK, hidden_split, D)
        pre_act = jnp.einsum("bd,dth->tbh", input_rows.astype(jnp.float32), first_groups)
        gelu_value, gelu_slope = gelu_parts(pre_act)
        hidden = gelu_value.astype(jnp.bfloat16).astype(jnp.float32)
        slot_output = group_total(jnp.einsum("tbh,thd->tbd", hidden, second_groups))
        hidden_grad = jnp.einsum("bd,thd->tbh", grad_rows.astype(jnp.float32), second_groups)
        pre_grad = (hidden_grad * gelu_slope).astype(jnp.bfloat16).astype(jnp.float32)
        slot_back = group_total(jnp.einsum("tbh,dth->tbd", pre_grad, first_groups))
        return slot_output, slot_back

    slot_output, slot_back = lax.map(expert_step, (jnp.transpose(slot_input, (1, 0, 2)), jnp.transpose(slot_grad, (1, 0, 2)), w_in, w_out))
    slot_output = jnp.transpose(slot_output, (1, 0, 2))
    slot_back = jnp.transpose(slot_back, (1, 0, 2))

    def token_backward(items):
        tok_image, grad_image, disp_image, comb_image, output_image, back_image = items
        comb_grad = jnp.dot(grad_image, output_image.T, preferred_element_type=jnp.float32)
        disp_grad = jnp.dot(tok_image, back_image.T, preferred_element_type=jnp.float32)
        comb_full = comb_image.astype(jnp.float32)
        disp_full = disp_image.astype(jnp.float32)
        comb_logit = comb_full * (comb_grad - jnp.sum(comb_full * comb_grad, axis=1, keepdims=True))
        totals = jnp.sum(disp_full * disp_grad, axis=0, keepdims=True)
        disp_logit = disp_full * (disp_grad - totals)
        logit_grad = (comb_logit + disp_logit).astype(jnp.bfloat16)
        result = jnp.dot(disp_image, back_image, preferred_element_type=jnp.float32)
        result = result + jnp.dot(logit_grad, slot_keys.T, preferred_element_type=jnp.float32)
        return result.astype(jnp.bfloat16)

    return lax.map(token_backward, (tokens, upstream, dispatch, combine, slot_output, slot_back))
```

```python
import jax
import jax.numpy as jnp
from jax import lax
from jax.experimental import pallas as pl
from jax.experimental.pallas import tpu as pltpu
from jax.sharding import Mesh
from jax.sharding import PartitionSpec as P

F32 = jnp.float32
BF16 = jnp.bfloat16
VMEM = pltpu.VMEM
MIB = 1024 * 1024


def dot(a, b, dims):
    return lax.dot_general(a, b, (dims, ((), ())), preferred_element_type=F32)


def slot_sums(disp_hbm, comb_hbm, tok_hbm, up_hbm, out_ref, disp_ref, comb_ref, tok_ref, up_ref, sems):
    quarters, _, both = out_ref.shape
    width = both // 2
    inputs = ((disp_hbm, disp_ref, tok_hbm, tok_ref), (comb_hbm, comb_ref, up_hbm, up_ref))
    copies = []
    for k, (weight_hbm, weight_ref, _, _) in enumerate(inputs):
        copies.append(pltpu.make_async_copy(weight_hbm, weight_ref, sems.at[quarters, k]))
    for q in range(quarters):
        cols = pl.ds(q * width, width)
        for k, (_, _, src, dst) in enumerate(inputs):
            copies.append(pltpu.make_async_copy(src.at[:, cols], dst.at[:, cols], sems.at[q, k]))
    for copy in copies:
        copy.start()
    weights = []
    for k in range(2):
        copies[k].wait()
        weights.append(inputs[k][1][...].T)
    for q in range(quarters):
        for k, (_, _, _, src) in enumerate(inputs):
            copies[2 + 2 * q + k].wait()
            part = dot(weights[k], src[:, q * width : (q + 1) * width], ((1,), (0,)))
            out_ref[q, :, k * width : (k + 1) * width] = part.astype(BF16)


def gelu_parts(pre_act):
    inside = 0.7978845608 * (pre_act + 0.044715 * pre_act * pre_act * pre_act)
    tanh_val = jnp.tanh(inside)
    gelu_value = 0.5 * pre_act * (1.0 + tanh_val)
    gelu_slope = 0.5 * (1.0 + tanh_val) + 0.5 * pre_act * (
        1.0 - tanh_val * tanh_val
    ) * 0.7978845608 * (1.0 + 3.0 * 0.044715 * pre_act * pre_act)
    return gelu_value, gelu_slope


def expert(rows_ref, first_ref, second_ref, out_ref):
    quarters, _, both = rows_ref.shape
    width = both // 2
    pre_act = hidden_grad = 0.0
    for q in range(quarters):
        cols = slice(q * width, (q + 1) * width)
        pre_act += dot(rows_ref[q, :, :width], first_ref[cols, :], ((1,), (0,)))
        hidden_grad += dot(rows_ref[q, :, width:], second_ref[:, cols], ((1,), (1,)))
    value, slope = gelu_parts(pre_act)
    hidden = value.astype(BF16)
    pre_grad = (hidden_grad * slope).astype(BF16)
    for q in range(quarters):
        cols = slice(q * width, (q + 1) * width)
        out_ref[q, :, :width] = dot(hidden, second_ref[:, cols], ((1,), (0,))).astype(BF16)
        out_ref[q, :, width:] = dot(pre_grad, first_ref[cols, :], ((1,), (1,))).astype(BF16)


def with_totals(back_ref, slots_ref, out_ref):
    rows, both = back_ref.shape
    width = both // 2
    out_ref[:rows, :] = back_ref[...]
    product = slots_ref[:, :width].astype(F32) * back_ref[:, width:].astype(F32)
    high = product.astype(BF16)
    low = (product - high.astype(F32)).astype(BF16)
    ones = jnp.ones((16, width), BF16)
    total = dot(ones, high, ((1,), (1,))) + dot(ones, low, ((1,), (1,)))
    total_high = total.astype(BF16)
    out_ref[rows:, :rows] = total_high
    out_ref[rows:, rows : 2 * rows] = (total - total_high.astype(F32)).astype(BF16)
    out_ref[rows:, 2 * rows :] = jnp.zeros((16, both - 2 * rows), BF16)


def tokens_back(rows_ref, tok_ref, up_ref, disp_ref, comb_ref, keys_ref, out_hbm, out_ref, sems):
    quarters, _, both = rows_ref.shape
    slots = disp_ref.shape[1]
    width = both // 2
    comb_grad = disp_grad = totals = 0.0
    for q in range(quarters):
        cols = slice(q * width, (q + 1) * width)
        comb_grad += dot(up_ref[:, cols], rows_ref[q, :slots, :width], ((1,), (1,)))
        disp_grad += dot(tok_ref[:, cols], rows_ref[q, :slots, width:], ((1,), (1,)))
        totals += rows_ref[q, slots:, :slots].astype(F32)
        totals += rows_ref[q, slots:, slots : 2 * slots].astype(F32)
    comb = comb_ref[...].astype(F32)
    disp = disp_ref[...].astype(F32)
    logit = comb * (comb_grad - jnp.sum(comb * comb_grad, axis=1, keepdims=True))
    logit += disp * (disp_grad - totals[:1, :])
    logit = logit.astype(BF16)
    copies = []
    for q in range(quarters):
        cols = slice(q * width, (q + 1) * width)
        part = dot(disp_ref[...], rows_ref[q, :slots, width:], ((1,), (0,)))
        part += dot(logit, keys_ref[cols, :], ((1,), (1,)))
        out_ref[:, cols] = part.astype(BF16)
        block = pl.ds(q * width, width)
        copy = pltpu.make_async_copy(out_ref.at[:, block], out_hbm.at[:, block], sems.at[q])
        copy.start()
        copies.append(copy)
    for copy in copies:
        copy.wait()


def vmem(count):
    return [pl.BlockSpec(memory_space=VMEM)] * count


def hbm(count):
    return [pl.BlockSpec(memory_space=pltpu.HBM)] * count


def params(mib):
    return pltpu.CompilerParams(vmem_limit_bytes=mib * MIB)


def tok_sum(parts, xl, core):
    given = lax.dynamic_index_in_dim(parts, 1 - core, 1, keepdims=False)
    kept = lax.dynamic_index_in_dim(parts, core, 1, keepdims=False)
    arrived = lax.all_gather(given, "core", axis=0)
    arrived = lax.dynamic_index_in_dim(arrived, 1 - core, 0, keepdims=False)

    def half(at):
        return sum(
            lax.dynamic_index_in_dim(v, at, 0, keepdims=False).astype(F32) for v in (kept, arrived)
        )

    across = lax.all_gather(half(1 - xl).astype(BF16), "x_lo", axis=0)
    across = lax.dynamic_index_in_dim(across, 1 - xl, 0, keepdims=False)
    return half(xl) + across.astype(F32)


EXP = ("y", "x_hi", "z")
TOK = ("x_lo", "core")


def exchanged(value):
    rows, cols = value.shape
    blocks = value.reshape(rows, cols // 128, 128)
    return lax.all_to_all(blocks, EXP, split_axis=0, concat_axis=0, tiled=True).reshape(rows, cols)


def body(tokens, upstream, dispatch, combine, w_in, w_out, slot_keys):
    tokens, upstream, dispatch, combine = tokens[0], upstream[0], dispatch[0], combine[0]
    rows, features = tokens.shape
    slots = dispatch.shape[1]
    quarters = 4
    width = features // quarters
    both = 2 * width
    xl, core = lax.axis_index("x_lo"), lax.axis_index("core")
    parts = jax.ShapeDtypeStruct((quarters, slots, both), BF16)

    partial = pl.pallas_call(
        slot_sums,
        out_shape=parts,
        in_specs=hbm(4),
        out_specs=vmem(1)[0],
        scratch_shapes=[
            VMEM((rows, slots), BF16),
            VMEM((rows, slots), BF16),
            VMEM((rows, features), BF16),
            VMEM((rows, features), BF16),
            pltpu.SemaphoreType.DMA((quarters + 1, 2)),
        ],
        compiler_params=params(53),
        name="slot_sums",
    )(dispatch, combine, tokens, upstream)
    summed = tok_sum(partial.reshape(2, 2, slots, both), xl, core).astype(BF16)
    arrived = exchanged(summed)
    images = arrived.shape[0]
    arrived = lax.all_gather(arrived, TOK, axis=0)

    leaving = pl.pallas_call(
        expert,
        out_shape=jax.ShapeDtypeStruct((quarters, images, both), BF16),
        in_specs=vmem(3),
        out_specs=vmem(1)[0],
        compiler_params=params(12),
        name="expert",
    )(arrived, w_in[0], w_out[0])
    leaving = tok_sum(leaving.reshape(2, 2, images, both), xl, core).astype(BF16)
    returned = exchanged(leaving)
    returned = pl.pallas_call(
        with_totals,
        out_shape=jax.ShapeDtypeStruct((slots + 16, both), BF16),
        in_specs=vmem(2),
        out_specs=vmem(1)[0],
        compiler_params=params(4),
        name="with_totals",
    )(returned, summed)
    returned = lax.all_gather(returned, TOK, axis=0)

    result = pl.pallas_call(
        tokens_back,
        out_shape=jax.ShapeDtypeStruct((rows, features), BF16),
        in_specs=vmem(6),
        out_specs=hbm(1)[0],
        scratch_shapes=[VMEM((rows, features), BF16), pltpu.SemaphoreType.DMA((quarters,))],
        compiler_params=params(12),
        name="tokens_back",
    )(returned, tokens, upstream, dispatch, combine, slot_keys)
    return result[None]


def solution(mesh):
    sizes = (2, 2, 4, 2, 16)
    fine = Mesh(mesh.devices.reshape(sizes), TOK + EXP)
    placed = (
        P(EXP, TOK, None),
        P(EXP, TOK, None),
        P(EXP, TOK, None),
        P(EXP, TOK, None),
        P(EXP, None, TOK),
        P(EXP, TOK, None),
        P(),
    )
    return jax.shard_map(
        body, mesh=fine, in_specs=placed, out_specs=P(EXP, TOK, None), check_vma=False
    )
```

```python
import jax
import jax.numpy as jnp
from jax import lax
from jax.experimental import pallas as pl
from jax.experimental.pallas import tpu as pltpu
from jax.sharding import Mesh
from jax.sharding import PartitionSpec as P

F32 = jnp.float32
BF16 = jnp.bfloat16
VMEM = pltpu.VMEM
MIB = 1024 * 1024


def dot(a, b, dims):
    return lax.dot_general(a, b, (dims, ((), ())), preferred_element_type=F32)


def opening(out_ref):
    out_ref[...] = jnp.zeros_like(out_ref)


def slot_sums(_, disp_ref, comb_ref, tok_ref, up_ref, out_ref):
    quarters, _, both = out_ref.shape
    width = both // 2
    for k, (weight, src) in enumerate(((disp_ref, tok_ref), (comb_ref, up_ref))):
        weight = weight[...].T
        for q in range(quarters):
            part = dot(weight, src[:, q * width : (q + 1) * width], ((1,), (0,)))
            out_ref[q, :, k * width : (k + 1) * width] = part.astype(BF16)


def gelu_parts(pre_act):
    inside = 0.7978845608 * (pre_act + 0.044715 * pre_act * pre_act * pre_act)
    tanh_val = jnp.tanh(inside)
    gelu_value = 0.5 * pre_act * (1.0 + tanh_val)
    gelu_slope = 0.5 * (1.0 + tanh_val) + 0.5 * pre_act * (
        1.0 - tanh_val * tanh_val
    ) * 0.7978845608 * (1.0 + 3.0 * 0.044715 * pre_act * pre_act)
    return gelu_value, gelu_slope


def expert(rows_ref, first_ref, second_ref, out_ref):
    quarters, _, both = rows_ref.shape
    width = both // 2
    pre_act = hidden_grad = 0.0
    for q in range(quarters):
        cols = slice(q * width, (q + 1) * width)
        pre_act += dot(rows_ref[q, :, :width], first_ref[cols, :], ((1,), (0,)))
        hidden_grad += dot(rows_ref[q, :, width:], second_ref[:, cols], ((1,), (1,)))
    value, slope = gelu_parts(pre_act)
    hidden = value.astype(BF16)
    pre_grad = (hidden_grad * slope).astype(BF16)
    for q in range(quarters):
        cols = slice(q * width, (q + 1) * width)
        out_ref[q, :, :width] = dot(hidden, second_ref[:, cols], ((1,), (0,))).astype(BF16)
        out_ref[q, :, width:] = dot(pre_grad, first_ref[cols, :], ((1,), (1,))).astype(BF16)


def transposed_rows(rows, inner):
    outer = rows // inner
    to = lax.broadcasted_iota(jnp.int32, (rows, rows), 0)
    at = lax.broadcasted_iota(jnp.int32, (rows, rows), 1)
    return (at == (to % outer) * inner + to // outer).astype(BF16)


def plane_sum(rows_ref, out_ref):
    rows = out_ref.shape[0]
    order = transposed_rows(rows, 16)
    total = dot(order, rows_ref[:rows, :], ((1,), (0,)))
    total += dot(order, rows_ref[rows:, :], ((1,), (0,)))
    out_ref[...] = total.astype(BF16)


def with_totals(back_ref, slots_ref, out_ref):
    rows, both = back_ref.shape
    width = both // 2
    order = transposed_rows(rows, rows // 16)
    back = dot(order, back_ref[...], ((1,), (0,)))
    out_ref[:rows, :] = back.astype(BF16)
    product = slots_ref[:, :width].astype(F32) * back[:, width:]
    high = product.astype(BF16)
    low = (product - high.astype(F32)).astype(BF16)
    ones = jnp.ones((16, width), BF16)
    total = dot(ones, high, ((1,), (1,))) + dot(ones, low, ((1,), (1,)))
    total_high = total.astype(BF16)
    out_ref[rows:, :rows] = total_high
    out_ref[rows:, rows : 2 * rows] = (total - total_high.astype(F32)).astype(BF16)
    out_ref[rows:, 2 * rows :] = jnp.zeros((16, both - 2 * rows), BF16)


def tokens_back(rows_ref, tok_ref, up_ref, disp_ref, comb_ref, keys_ref, out_hbm, out_ref, sems):
    quarters, _, both = rows_ref.shape
    slots = disp_ref.shape[1]
    width = both // 2
    comb_grad = disp_grad = totals = 0.0
    for q in range(quarters):
        cols = slice(q * width, (q + 1) * width)
        comb_grad += dot(up_ref[:, cols], rows_ref[q, :slots, :width], ((1,), (1,)))
        disp_grad += dot(tok_ref[:, cols], rows_ref[q, :slots, width:], ((1,), (1,)))
        totals += rows_ref[q, slots:, :slots].astype(F32)
        totals += rows_ref[q, slots:, slots : 2 * slots].astype(F32)
    comb = comb_ref[...].astype(F32)
    disp = disp_ref[...].astype(F32)
    logit = comb * (comb_grad - jnp.sum(comb * comb_grad, axis=1, keepdims=True))
    logit += disp * (disp_grad - totals[:1, :])
    logit = logit.astype(BF16)
    copies = []
    for q in range(quarters):
        cols = slice(q * width, (q + 1) * width)
        part = dot(disp_ref[...], rows_ref[q, :slots, width:], ((1,), (0,)))
        part += dot(logit, keys_ref[cols, :], ((1,), (1,)))
        out_ref[:, cols] = part.astype(BF16)
        block = pl.ds(q * width, width)
        copy = pltpu.make_async_copy(out_ref.at[:, block], out_hbm.at[:, block], sems.at[q])
        copy.start()
        copies.append(copy)
    for copy in copies:
        copy.wait()


def vmem(count):
    return [pl.BlockSpec(memory_space=VMEM)] * count


def params(mib):
    return pltpu.CompilerParams(vmem_limit_bytes=mib * MIB)


def pick(value, at, dim=0):
    return lax.dynamic_index_in_dim(value, at, dim, keepdims=False)


def core_terms(parts, core):
    given = pick(parts, 1 - core, 1)
    arrived = lax.all_gather(given, "core", axis=0)
    return pick(parts, core, 1), pick(arrived, 1 - core)


def tok_sum(parts, xl, core):
    terms = core_terms(parts, core)

    def half(at):
        return sum(pick(v, at).astype(F32) for v in terms)

    across = lax.all_gather(half(1 - xl).astype(BF16), "x_lo", axis=0)
    return half(xl) + pick(across, 1 - xl).astype(F32)


EXP = ("y", "x_hi", "z")
TOK = ("x_lo", "core")


def exchanged(value):
    rows, cols = value.shape
    blocks = value.reshape(rows, cols // 128, 128)
    return lax.all_to_all(blocks, EXP, split_axis=0, concat_axis=0, tiled=True).reshape(rows, cols)


def body(tokens, upstream, dispatch, combine, w_in, w_out, slot_keys):
    tokens, upstream, dispatch, combine = tokens[0], upstream[0], dispatch[0], combine[0]
    rows, features = tokens.shape
    slots = dispatch.shape[1]
    quarters = 4
    width = features // quarters
    both = 2 * width
    xl, core = lax.axis_index("x_lo"), lax.axis_index("core")
    parts = jax.ShapeDtypeStruct((quarters, slots, both), BF16)

    opened = pl.pallas_call(
        opening,
        out_shape=jax.ShapeDtypeStruct((8, 128), F32),
        out_specs=vmem(1)[0],
        compiler_params=params(1),
        cost_estimate=pl.CostEstimate(flops=10**10, bytes_accessed=10**7, transcendentals=0),
        name="opening",
    )()
    partial = pl.pallas_call(
        slot_sums,
        out_shape=parts,
        in_specs=vmem(5),
        out_specs=vmem(1)[0],
        compiler_params=params(8),
        name="slot_sums",
    )(opened, dispatch, combine, tokens, upstream)
    summed = tok_sum(partial.reshape(2, 2, slots, both), xl, core).astype(BF16)
    arrived = exchanged(summed)
    images = arrived.shape[0]
    arrived = lax.all_gather(arrived, TOK, axis=0)

    leaving = pl.pallas_call(
        expert,
        out_shape=jax.ShapeDtypeStruct((quarters, images, both), BF16),
        in_specs=vmem(3),
        out_specs=vmem(1)[0],
        compiler_params=params(12),
        name="expert",
    )(arrived, w_in[0], w_out[0])
    terms = core_terms(leaving.reshape(2, 2, images, both), core)
    leaving = sum(v.astype(F32) for v in terms).astype(BF16)
    plane = ("x_lo", "y", "x_hi")
    leaving = lax.all_to_all(leaving.reshape(16, 16, both), plane, 0, 0, tiled=True)
    leaving = pl.pallas_call(
        plane_sum,
        out_shape=jax.ShapeDtypeStruct((slots, both), BF16),
        in_specs=vmem(1),
        out_specs=vmem(1)[0],
        compiler_params=params(4),
        name="plane_sum",
    )(leaving.reshape(2 * slots, both))
    leaving = leaving.reshape(16, slots // 16, both)
    returned = lax.all_to_all(leaving, "z", 0, 0, tiled=True).reshape(slots, both)
    returned = pl.pallas_call(
        with_totals,
        out_shape=jax.ShapeDtypeStruct((slots + 16, both), BF16),
        in_specs=vmem(2),
        out_specs=vmem(1)[0],
        compiler_params=params(4),
        name="with_totals",
    )(returned, summed)
    returned = lax.all_gather(returned, TOK, axis=0)

    result = pl.pallas_call(
        tokens_back,
        out_shape=jax.ShapeDtypeStruct((rows, features), BF16),
        in_specs=vmem(6),
        out_specs=pl.BlockSpec(memory_space=pl.ANY),
        scratch_shapes=[VMEM((rows, features), BF16), pltpu.SemaphoreType.DMA((quarters,))],
        compiler_params=params(12),
        name="tokens_back",
    )(returned, tokens, upstream, dispatch, combine, slot_keys)
    return result[None]


def solution(mesh):
    sizes = (2, 2, 4, 2, 16)
    fine = Mesh(mesh.devices.reshape(sizes), TOK + EXP)
    placed = (
        P(EXP, TOK, None),
        P(EXP, TOK, None),
        P(EXP, TOK, None),
        P(EXP, TOK, None),
        P(EXP, None, TOK),
        P(EXP, TOK, None),
        P(),
    )
    return jax.shard_map(
        body, mesh=fine, in_specs=placed, out_specs=P(EXP, TOK, None), check_vma=False
    )
```

```python
import jax
import jax.numpy as jnp
from jax import lax
from jax.experimental import pallas as pl
from jax.experimental.pallas import tpu as pltpu
from jax.sharding import Mesh
from jax.sharding import PartitionSpec as P

F32 = jnp.float32
BF16 = jnp.bfloat16
VMEM = pltpu.VMEM
MIB = 1024 * 1024


def dot(a, b, dims):
    return lax.dot_general(a, b, (dims, ((), ())), preferred_element_type=F32)


def opening(out_ref):
    out_ref[...] = jnp.zeros_like(out_ref)


def slot_sums(_, disp_ref, comb_ref, tok_ref, up_ref, out_ref):
    quarters, _, both = out_ref.shape
    width = both // 2
    for k, (weight, src) in enumerate(((disp_ref, tok_ref), (comb_ref, up_ref))):
        weight = weight[...].T
        for q in range(quarters):
            part = dot(weight, src[:, q * width : (q + 1) * width], ((1,), (0,)))
            out_ref[q, :, k * width : (k + 1) * width] = part.astype(BF16)


def gelu_parts(pre_act):
    inside = 0.7978845608 * (pre_act + 0.044715 * pre_act * pre_act * pre_act)
    tanh_val = jnp.tanh(inside)
    gelu_value = 0.5 * pre_act * (1.0 + tanh_val)
    gelu_slope = 0.5 * (1.0 + tanh_val) + 0.5 * pre_act * (
        1.0 - tanh_val * tanh_val
    ) * 0.7978845608 * (1.0 + 3.0 * 0.044715 * pre_act * pre_act)
    return gelu_value, gelu_slope


def transposed_rows(rows, inner):
    outer = rows // inner
    to = lax.broadcasted_iota(jnp.int32, (rows, rows), 0)
    at = lax.broadcasted_iota(jnp.int32, (rows, rows), 1)
    return (at == (to % outer) * inner + to // outer).astype(BF16)


def expert(rows_ref, first_ref, second_ref, out_ref):
    quarters, images, both = out_ref.shape
    width = both // 2
    order = transposed_rows(images, images // 16)
    pre_act = hidden_grad = 0.0
    for q in range(quarters):
        cols = slice(q * width, (q + 1) * width)
        rows = dot(order, rows_ref[q, :, :both], ((1,), (0,))).astype(BF16)
        pre_act += dot(rows[:, :width], first_ref[cols, :], ((1,), (0,)))
        hidden_grad += dot(rows[:, width:], second_ref[:, cols], ((1,), (1,)))
    value, slope = gelu_parts(pre_act)
    hidden = value.astype(BF16)
    pre_grad = (hidden_grad * slope).astype(BF16)
    for q in range(quarters):
        cols = slice(q * width, (q + 1) * width)
        out_ref[q, :, :width] = dot(hidden, second_ref[:, cols], ((1,), (0,))).astype(BF16)
        out_ref[q, :, width:] = dot(pre_grad, first_ref[cols, :], ((1,), (1,))).astype(BF16)


def plane_sum(rows_ref, out_ref):
    rows = out_ref.shape[0]
    order = transposed_rows(rows, 16)
    total = dot(order, rows_ref[:rows, :], ((1,), (0,)))
    total += dot(order, rows_ref[rows:, :], ((1,), (0,)))
    out_ref[...] = total.astype(BF16)


def with_totals(back_ref, slots_ref, out_ref):
    rows, both = back_ref.shape
    width = both // 2
    order = transposed_rows(rows, rows // 16)
    back = dot(order, back_ref[...], ((1,), (0,)))
    out_ref[:rows, :] = back.astype(BF16)
    product = slots_ref[...] * back[:, width:]
    high = product.astype(BF16)
    low = (product - high.astype(F32)).astype(BF16)
    ones = jnp.ones((16, width), BF16)
    total = dot(ones, high, ((1,), (1,))) + dot(ones, low, ((1,), (1,)))
    total_high = total.astype(BF16)
    out_ref[rows:, :rows] = total_high
    out_ref[rows:, rows : 2 * rows] = (total - total_high.astype(F32)).astype(BF16)
    out_ref[rows:, 2 * rows :] = jnp.zeros((16, both - 2 * rows), BF16)


def tokens_back(rows_ref, tok_ref, up_ref, disp_ref, comb_ref, keys_ref, out_hbm, out_ref, sems):
    quarters, _, both = rows_ref.shape
    slots = disp_ref.shape[1]
    width = both // 2
    comb_grad = disp_grad = totals = 0.0
    for q in range(quarters):
        cols = slice(q * width, (q + 1) * width)
        comb_grad += dot(up_ref[:, cols], rows_ref[q, :slots, :width], ((1,), (1,)))
        disp_grad += dot(tok_ref[:, cols], rows_ref[q, :slots, width:], ((1,), (1,)))
        totals += rows_ref[q, slots:, :slots].astype(F32)
        totals += rows_ref[q, slots:, slots : 2 * slots].astype(F32)
    comb = comb_ref[...].astype(F32)
    disp = disp_ref[...].astype(F32)
    logit = comb * (comb_grad - jnp.sum(comb * comb_grad, axis=1, keepdims=True))
    logit += disp * (disp_grad - totals[:1, :])
    logit = logit.astype(BF16)
    copies = []
    for q in range(quarters):
        cols = slice(q * width, (q + 1) * width)
        part = dot(disp_ref[...], rows_ref[q, :slots, width:], ((1,), (0,)))
        part += dot(logit, keys_ref[cols, :], ((1,), (1,)))
        out_ref[:, cols] = part.astype(BF16)
        block = pl.ds(q * width, width)
        copy = pltpu.make_async_copy(out_ref.at[:, block], out_hbm.at[:, block], sems.at[q])
        copy.start()
        copies.append(copy)
    for copy in copies:
        copy.wait()


def vmem(count):
    return [pl.BlockSpec(memory_space=VMEM)] * count


def params(mib):
    return pltpu.CompilerParams(vmem_limit_bytes=mib * MIB)


def pick(value, at, dim=0):
    return lax.dynamic_index_in_dim(value, at, dim, keepdims=False)


TOK = ("x_lo", "core")
PLANE = ("x_lo", "y", "x_hi")
EXP = ("y", "x_hi", "z")


def chip_sum(parts, core):
    parts = parts.reshape(2, 2, *parts.shape[1:])
    arrived = lax.all_gather(pick(parts, 1 - core, 1), "core", axis=0)
    terms = (pick(parts, core, 1), pick(arrived, 1 - core))
    return sum(v.astype(F32) for v in terms).astype(BF16)


def exchanged(value):
    halves, rows, both = value.shape
    value = value.reshape(halves * rows // 16, 16, both)
    value = lax.all_to_all(value, PLANE, 0, 0, tiled=True)
    value = pl.pallas_call(
        plane_sum,
        out_shape=jax.ShapeDtypeStruct((rows, both), BF16),
        in_specs=vmem(1),
        out_specs=vmem(1)[0],
        compiler_params=params(4),
        name="plane_sum",
    )(value.reshape(halves * rows, both))
    value = value.reshape(16, rows // 16, both)
    return lax.all_to_all(value, "z", 0, 0, tiled=True).reshape(rows, both)


def body(tokens, upstream, dispatch, combine, w_in, w_out, slot_keys):
    tokens, upstream, dispatch, combine = tokens[0], upstream[0], dispatch[0], combine[0]
    rows, features = tokens.shape
    slots = dispatch.shape[1]
    quarters = 4
    width = features // quarters
    both = 2 * width
    xl, core = (lax.axis_index(axis).astype(jnp.uint32) for axis in TOK)
    partner = 2 * (1 - xl) + core
    across = 1 - xl
    parts = jax.ShapeDtypeStruct((quarters, slots, both), BF16)

    opened = pl.pallas_call(
        opening,
        out_shape=jax.ShapeDtypeStruct((8, 128), F32),
        out_specs=vmem(1)[0],
        compiler_params=params(1),
        cost_estimate=pl.CostEstimate(flops=10**10, bytes_accessed=10**7, transcendentals=0),
        name="opening",
    )()
    partial = pl.pallas_call(
        slot_sums,
        out_shape=parts,
        in_specs=vmem(5),
        out_specs=vmem(1)[0],
        compiler_params=params(8),
        name="slot_sums",
    )(opened, dispatch, combine, tokens, upstream)
    held = (partial, xl, across, core, partner)
    partial, xl, across, core, partner = lax.optimization_barrier(held)
    sums = lax.optimization_barrier(chip_sum(partial, core))
    arrived, sums = lax.optimization_barrier((exchanged(sums), sums))
    images = arrived.shape[0]
    spare = pick(sums, across)[:, :width]
    arrived = lax.all_gather(jnp.concatenate([arrived, spare], axis=1), TOK, axis=0)
    other = pick(arrived, partner)[:, both:]
    slot_input = pick(sums, xl)[:, :width].astype(F32) + other.astype(F32)
    arrived, slot_input = lax.optimization_barrier((arrived, slot_input))

    leaving = pl.pallas_call(
        expert,
        out_shape=jax.ShapeDtypeStruct((quarters, images, both), BF16),
        in_specs=vmem(3),
        out_specs=vmem(1)[0],
        compiler_params=params(12),
        name="expert",
    )(arrived, w_in[0], w_out[0])
    returned = exchanged(chip_sum(leaving, core))
    returned = pl.pallas_call(
        with_totals,
        out_shape=jax.ShapeDtypeStruct((slots + 16, both), BF16),
        in_specs=vmem(2),
        out_specs=vmem(1)[0],
        compiler_params=params(4),
        name="with_totals",
    )(returned, slot_input)
    returned = lax.all_gather(returned, TOK, axis=0)

    result = pl.pallas_call(
        tokens_back,
        out_shape=jax.ShapeDtypeStruct((rows, features), BF16),
        in_specs=vmem(6),
        out_specs=pl.BlockSpec(memory_space=pl.ANY),
        scratch_shapes=[VMEM((rows, features), BF16), pltpu.SemaphoreType.DMA((quarters,))],
        compiler_params=params(12),
        name="tokens_back",
    )(returned, tokens, upstream, dispatch, combine, slot_keys)
    return result[None]


def solution(mesh):
    sizes = (2, 2, 4, 2, 16)
    fine = Mesh(mesh.devices.reshape(sizes), TOK + EXP)
    placed = (
        P(EXP, TOK, None),
        P(EXP, TOK, None),
        P(EXP, TOK, None),
        P(EXP, TOK, None),
        P(EXP, None, TOK),
        P(EXP, TOK, None),
        P(),
    )
    return jax.shard_map(
        body, mesh=fine, in_specs=placed, out_specs=P(EXP, TOK, None), check_vma=False
    )
```

```python
import jax
import jax.numpy as jnp
from jax import lax
from jax.experimental import pallas as pl
from jax.experimental.pallas import tpu as pltpu
from jax.sharding import Mesh
from jax.sharding import PartitionSpec as P

F32 = jnp.float32
BF16 = jnp.bfloat16
VMEM = pltpu.VMEM
MIB = 1024 * 1024


def dot(a, b, dims):
    return lax.dot_general(a, b, (dims, ((), ())), preferred_element_type=F32)


def opening(out_ref):
    out_ref[...] = jnp.zeros_like(out_ref)


def slot_sums(_, disp_ref, comb_ref, tok_ref, up_ref, out_ref):
    quarters, _, both = out_ref.shape
    width = both // 2
    for k, (weight, src) in enumerate(((disp_ref, tok_ref), (comb_ref, up_ref))):
        weight = weight[...].T
        for q in range(quarters):
            part = dot(weight, src[:, q * width : (q + 1) * width], ((1,), (0,)))
            out_ref[q, :, k * width : (k + 1) * width] = part.astype(BF16)


def gelu_parts(pre_act):
    inside = 0.7978845608 * (pre_act + 0.044715 * pre_act * pre_act * pre_act)
    tanh_val = jnp.tanh(inside)
    gelu_value = 0.5 * pre_act * (1.0 + tanh_val)
    gelu_slope = 0.5 * (1.0 + tanh_val) + 0.5 * pre_act * (
        1.0 - tanh_val * tanh_val
    ) * 0.7978845608 * (1.0 + 3.0 * 0.044715 * pre_act * pre_act)
    return gelu_value, gelu_slope


def expert(rows_ref, first_ref, second_ref, out_ref):
    quarters, _, both = rows_ref.shape
    width = both // 2
    pre_act = hidden_grad = 0.0
    for q in range(quarters):
        cols = slice(q * width, (q + 1) * width)
        pre_act += dot(rows_ref[q, :, :width], first_ref[cols, :], ((1,), (0,)))
        hidden_grad += dot(rows_ref[q, :, width:], second_ref[:, cols], ((1,), (1,)))
    value, slope = gelu_parts(pre_act)
    hidden = value.astype(BF16)
    pre_grad = (hidden_grad * slope).astype(BF16)
    for q in range(quarters):
        cols = slice(q * width, (q + 1) * width)
        out_ref[q, :, :width] = dot(hidden, second_ref[:, cols], ((1,), (0,))).astype(BF16)
        out_ref[q, :, width:] = dot(pre_grad, first_ref[cols, :], ((1,), (1,))).astype(BF16)


def transposed_rows(rows, inner):
    outer = rows // inner
    to = lax.broadcasted_iota(jnp.int32, (rows, rows), 0)
    at = lax.broadcasted_iota(jnp.int32, (rows, rows), 1)
    return (at == (to % outer) * inner + to // outer).astype(BF16)


def plane_sum(rows_ref, out_ref):
    rows = out_ref.shape[0]
    order = transposed_rows(rows, 16)
    total = dot(order, rows_ref[:rows, :], ((1,), (0,)))
    total += dot(order, rows_ref[rows:, :], ((1,), (0,)))
    out_ref[...] = total.astype(BF16)


def with_totals(back_ref, slots_ref, out_ref):
    rows, both = back_ref.shape
    width = both // 2
    order = transposed_rows(rows, rows // 16)
    back = dot(order, back_ref[...], ((1,), (0,)))
    out_ref[:rows, :] = back.astype(BF16)
    product = slots_ref[:, :width].astype(F32) * back[:, width:]
    high = product.astype(BF16)
    low = (product - high.astype(F32)).astype(BF16)
    ones = jnp.ones((16, width), BF16)
    total = dot(ones, high, ((1,), (1,))) + dot(ones, low, ((1,), (1,)))
    total_high = total.astype(BF16)
    out_ref[rows:, :rows] = total_high
    out_ref[rows:, rows : 2 * rows] = (total - total_high.astype(F32)).astype(BF16)
    out_ref[rows:, 2 * rows :] = jnp.zeros((16, both - 2 * rows), BF16)


def tokens_back(rows_ref, tok_ref, up_ref, disp_ref, comb_ref, keys_ref, out_hbm, out_ref, sems):
    quarters, _, both = rows_ref.shape
    slots = disp_ref.shape[1]
    width = both // 2
    comb_grad = disp_grad = totals = 0.0
    for q in range(quarters):
        cols = slice(q * width, (q + 1) * width)
        comb_grad += dot(up_ref[:, cols], rows_ref[q, :slots, :width], ((1,), (1,)))
        disp_grad += dot(tok_ref[:, cols], rows_ref[q, :slots, width:], ((1,), (1,)))
        totals += rows_ref[q, slots:, :slots].astype(F32)
        totals += rows_ref[q, slots:, slots : 2 * slots].astype(F32)
    comb = comb_ref[...].astype(F32)
    disp = disp_ref[...].astype(F32)
    logit = comb * (comb_grad - jnp.sum(comb * comb_grad, axis=1, keepdims=True))
    logit += disp * (disp_grad - totals[:1, :])
    logit = logit.astype(BF16)
    copies = []
    for q in range(quarters):
        cols = slice(q * width, (q + 1) * width)
        part = dot(disp_ref[...], rows_ref[q, :slots, width:], ((1,), (0,)))
        part += dot(logit, keys_ref[cols, :], ((1,), (1,)))
        out_ref[:, cols] = part.astype(BF16)
        block = pl.ds(q * width, width)
        copy = pltpu.make_async_copy(out_ref.at[:, block], out_hbm.at[:, block], sems.at[q])
        copy.start()
        copies.append(copy)
    for copy in copies:
        copy.wait()


def vmem(count):
    return [pl.BlockSpec(memory_space=VMEM)] * count


def params(mib):
    return pltpu.CompilerParams(vmem_limit_bytes=mib * MIB)


def pick(value, at, dim=0):
    return lax.dynamic_index_in_dim(value, at, dim, keepdims=False)


def core_terms(parts, core):
    given = pick(parts, 1 - core, 1)
    arrived = lax.all_gather(given, "core", axis=0)
    return pick(parts, core, 1), pick(arrived, 1 - core)


def tok_sum(parts, xl, core):
    terms = core_terms(parts, core)

    def half(at):
        return sum(pick(v, at).astype(F32) for v in terms)

    across = lax.all_gather(half(1 - xl).astype(BF16), "x_lo", axis=0)
    return half(xl) + pick(across, 1 - xl).astype(F32)


EXP = ("y", "x_hi", "z")
TOK = ("x_lo", "core")


def exchanged(value):
    rows, cols = value.shape
    blocks = value.reshape(rows, cols // 128, 128)
    return lax.all_to_all(blocks, EXP, split_axis=0, concat_axis=0, tiled=True).reshape(rows, cols)


def body(tokens, upstream, dispatch, combine, w_in, w_out, slot_keys):
    tokens, upstream, dispatch, combine = tokens[0], upstream[0], dispatch[0], combine[0]
    rows, features = tokens.shape
    slots = dispatch.shape[1]
    quarters = 4
    width = features // quarters
    both = 2 * width
    xl, core = lax.axis_index("x_lo"), lax.axis_index("core")
    parts = jax.ShapeDtypeStruct((quarters, slots, both), BF16)

    opened = pl.pallas_call(
        opening,
        out_shape=jax.ShapeDtypeStruct((8, 128), F32),
        out_specs=vmem(1)[0],
        compiler_params=params(1),
        cost_estimate=pl.CostEstimate(flops=10**10, bytes_accessed=10**7, transcendentals=0),
        name="opening",
    )()
    partial = pl.pallas_call(
        slot_sums,
        out_shape=parts,
        in_specs=vmem(5),
        out_specs=vmem(1)[0],
        compiler_params=params(8),
        name="slot_sums",
    )(opened, dispatch, combine, tokens, upstream)
    summed = tok_sum(partial.reshape(2, 2, slots, both), xl, core).astype(BF16)
    arrived = exchanged(summed)
    images = arrived.shape[0]
    arrived, w_in, w_out = lax.optimization_barrier((arrived, w_in, w_out))
    arrived = lax.all_gather(arrived, TOK, axis=0)

    leaving = pl.pallas_call(
        expert,
        out_shape=jax.ShapeDtypeStruct((quarters, images, both), BF16),
        in_specs=vmem(3),
        out_specs=vmem(1)[0],
        compiler_params=params(12),
        name="expert",
    )(arrived, w_in[0], w_out[0])
    terms = core_terms(leaving.reshape(2, 2, images, both), core)
    leaving = sum(v.astype(F32) for v in terms).astype(BF16)
    plane = ("x_lo", "y", "x_hi")
    leaving = lax.all_to_all(leaving.reshape(16, 16, both), plane, 0, 0, tiled=True)
    leaving = pl.pallas_call(
        plane_sum,
        out_shape=jax.ShapeDtypeStruct((slots, both), BF16),
        in_specs=vmem(1),
        out_specs=vmem(1)[0],
        compiler_params=params(4),
        name="plane_sum",
    )(leaving.reshape(2 * slots, both))
    leaving = leaving.reshape(16, slots // 16, both)
    returned = lax.all_to_all(leaving, "z", 0, 0, tiled=True).reshape(slots, both)
    returned = pl.pallas_call(
        with_totals,
        out_shape=jax.ShapeDtypeStruct((slots + 16, both), BF16),
        in_specs=vmem(2),
        out_specs=vmem(1)[0],
        compiler_params=params(4),
        name="with_totals",
    )(returned, summed)
    returned = lax.all_gather(returned, TOK, axis=0)

    result = pl.pallas_call(
        tokens_back,
        out_shape=jax.ShapeDtypeStruct((rows, features), BF16),
        in_specs=vmem(6),
        out_specs=pl.BlockSpec(memory_space=pl.ANY),
        scratch_shapes=[VMEM((rows, features), BF16), pltpu.SemaphoreType.DMA((quarters,))],
        compiler_params=params(12),
        name="tokens_back",
    )(returned, tokens, upstream, dispatch, combine, slot_keys)
    return result[None]


def solution(mesh):
    sizes = (2, 2, 4, 2, 16)
    fine = Mesh(mesh.devices.reshape(sizes), TOK + EXP)
    placed = (
        P(EXP, TOK, None),
        P(EXP, TOK, None),
        P(EXP, TOK, None),
        P(EXP, TOK, None),
        P(EXP, None, TOK),
        P(EXP, TOK, None),
        P(),
    )
    return jax.shard_map(
        body, mesh=fine, in_specs=placed, out_specs=P(EXP, TOK, None), check_vma=False
    )
```

```python
import jax
import jax.numpy as jnp
from jax import lax
from jax.experimental import pallas as pl
from jax.experimental.pallas import tpu as pltpu
from jax.sharding import Mesh
from jax.sharding import PartitionSpec as P

F32 = jnp.float32
BF16 = jnp.bfloat16
VMEM = pltpu.VMEM
MIB = 1024 * 1024


def dot(a, b, dims):
    return lax.dot_general(a, b, (dims, ((), ())), preferred_element_type=F32)


def opening(out_ref):
    out_ref[...] = jnp.zeros_like(out_ref)


def slot_sums(_, disp_ref, comb_ref, tok_ref, up_ref, out_ref):
    quarters, _, both = out_ref.shape
    width = both // 2
    for k, (weight, src) in enumerate(((disp_ref, tok_ref), (comb_ref, up_ref))):
        weight = weight[...].T
        for q in range(quarters):
            part = dot(weight, src[:, q * width : (q + 1) * width], ((1,), (0,)))
            out_ref[q, :, k * width : (k + 1) * width] = part.astype(BF16)


def gelu_parts(pre_act):
    inside = 0.7978845608 * (pre_act + 0.044715 * pre_act * pre_act * pre_act)
    tanh_val = jnp.tanh(inside)
    gelu_value = 0.5 * pre_act * (1.0 + tanh_val)
    gelu_slope = 0.5 * (1.0 + tanh_val) + 0.5 * pre_act * (
        1.0 - tanh_val * tanh_val
    ) * 0.7978845608 * (1.0 + 3.0 * 0.044715 * pre_act * pre_act)
    return gelu_value, gelu_slope


def expert(place_ref, rows_ref, first_ref, second_ref, out_ref):
    quarters, images, both = rows_ref.shape
    width = both // 2
    pre_act = hidden_grad = total = 0.0
    for q in range(quarters):
        cols = slice(q * width, (q + 1) * width)
        pre_act += dot(rows_ref[q, :, :width], first_ref[cols, :], ((1,), (0,)))
        hidden_grad += dot(rows_ref[q, :, width:], second_ref[:, cols], ((1,), (1,)))
    value, slope = gelu_parts(pre_act)
    hidden = value.astype(BF16)
    pre_grad = (hidden_grad * slope).astype(BF16)
    for q in range(quarters):
        cols = slice(q * width, (q + 1) * width)
        out_ref[q, :, :width] = dot(hidden, second_ref[:, cols], ((1,), (0,))).astype(BF16)
        back = dot(pre_grad, first_ref[cols, :], ((1,), (1,))).astype(BF16)
        out_ref[q, :, width:both] = back
        total += rows_ref[q, :, :width].astype(F32) * back.astype(F32)
    total = jnp.sum(total, axis=1, keepdims=True)
    high = total.astype(BF16).astype(F32)
    extra = out_ref.shape[2] - both
    column = lax.broadcasted_iota(jnp.int32, (images, extra), 1) - 2 * place_ref[0]
    terms = jnp.where(column == 0, high, jnp.where(column == 1, total - high, 0.0)).astype(BF16)
    for q in range(quarters):
        out_ref[q, :, both:] = terms


def transposed_rows(rows, inner):
    outer = rows // inner
    to = lax.broadcasted_iota(jnp.int32, (rows, rows), 0)
    at = lax.broadcasted_iota(jnp.int32, (rows, rows), 1)
    return (at == (to % outer) * inner + to // outer).astype(BF16)


def plane_sum(rows_ref, out_ref):
    rows = out_ref.shape[0]
    order = transposed_rows(rows, 16)
    total = dot(order, rows_ref[:rows, :], ((1,), (0,)))
    total += dot(order, rows_ref[rows:, :], ((1,), (0,)))
    out_ref[...] = total.astype(BF16)


def in_order(rows_ref, out_ref):
    rows = out_ref.shape[0]
    order = transposed_rows(rows, rows // 16)
    out_ref[...] = dot(order, rows_ref[...], ((1,), (0,))).astype(BF16)


def in_order_with_totals(rows_ref, out_ref, totals_ref):
    rows, both = out_ref.shape
    order = transposed_rows(rows, rows // 16)
    out_ref[...] = dot(order, rows_ref[:, :both], ((1,), (0,))).astype(BF16)
    terms = dot(order, rows_ref[:, both:], ((1,), (0,))).astype(BF16)
    ones = jnp.ones((16, terms.shape[1]), BF16)
    totals_ref[...] = dot(ones, terms, ((1,), (1,)))[: totals_ref.shape[0]]


def tokens_back(rows_ref, totals_ref, tok_ref, up_ref, disp_ref, comb_ref, keys_ref, out_hbm, out_ref, sems):
    quarters, _, both = rows_ref.shape
    width = both // 2
    comb_grad = disp_grad = 0.0
    for q in range(quarters):
        cols = slice(q * width, (q + 1) * width)
        comb_grad += dot(up_ref[:, cols], rows_ref[q, :, :width], ((1,), (1,)))
        disp_grad += dot(tok_ref[:, cols], rows_ref[q, :, width:], ((1,), (1,)))
    comb = comb_ref[...].astype(F32)
    disp = disp_ref[...].astype(F32)
    logit = comb * (comb_grad - jnp.sum(comb * comb_grad, axis=1, keepdims=True))
    logit += disp * (disp_grad - totals_ref[:1, :])
    logit = logit.astype(BF16)
    copies = []
    for q in range(quarters):
        cols = slice(q * width, (q + 1) * width)
        part = dot(disp_ref[...], rows_ref[q, :, width:], ((1,), (0,)))
        part += dot(logit, keys_ref[cols, :], ((1,), (1,)))
        out_ref[:, cols] = part.astype(BF16)
        block = pl.ds(q * width, width)
        copy = pltpu.make_async_copy(out_ref.at[:, block], out_hbm.at[:, block], sems.at[q])
        copy.start()
        copies.append(copy)
    for copy in copies:
        copy.wait()


def vmem(count):
    return [pl.BlockSpec(memory_space=VMEM)] * count


def params(mib):
    return pltpu.CompilerParams(vmem_limit_bytes=mib * MIB)


def pick(value, at, dim=0):
    return lax.dynamic_index_in_dim(value, at, dim, keepdims=False)


TOK = ("x_lo", "core")
PLANE = ("x_lo", "y", "x_hi")
EXP = ("y", "x_hi", "z")


def chip_sum(parts, core):
    parts = parts.reshape(2, 2, *parts.shape[1:])
    arrived = lax.all_gather(pick(parts, 1 - core, 1), "core", axis=0)
    terms = (pick(parts, core, 1), pick(arrived, 1 - core))
    return sum(v.astype(F32) for v in terms).astype(BF16)


def exchanged(value):
    halves, rows, both = value.shape
    value = value.reshape(halves * rows // 16, 16, both)
    value = lax.all_to_all(value, PLANE, 0, 0, tiled=True)
    value = pl.pallas_call(
        plane_sum,
        out_shape=jax.ShapeDtypeStruct((rows, both), BF16),
        in_specs=vmem(1),
        out_specs=vmem(1)[0],
        compiler_params=params(4),
        name="plane_sum",
    )(value.reshape(halves * rows, both))
    value = value.reshape(16, rows // 16, both)
    return lax.all_to_all(value, "z", 0, 0, tiled=True).reshape(rows, both)


def body(tokens, upstream, dispatch, combine, w_in, w_out, slot_keys):
    tokens, upstream, dispatch, combine = tokens[0], upstream[0], dispatch[0], combine[0]
    rows, features = tokens.shape
    slots = dispatch.shape[1]
    quarters = 4
    width = features // quarters
    both = 2 * width
    core = lax.axis_index("core").astype(jnp.uint32)
    place = lax.axis_index(TOK).reshape(1)
    opened = pl.pallas_call(
        opening,
        out_shape=jax.ShapeDtypeStruct((8, 128), F32),
        out_specs=vmem(1)[0],
        compiler_params=params(1),
        cost_estimate=pl.CostEstimate(flops=10**10, bytes_accessed=10**7, transcendentals=0),
        name="opening",
    )()
    partial = pl.pallas_call(
        slot_sums,
        out_shape=jax.ShapeDtypeStruct((quarters, slots, both), BF16),
        in_specs=vmem(5),
        out_specs=vmem(1)[0],
        compiler_params=params(8),
        name="slot_sums",
    )(opened, dispatch, combine, tokens, upstream)
    partial, core, place = lax.optimization_barrier((partial, core, place))
    arrived = exchanged(chip_sum(partial, core))
    images = arrived.shape[0]
    arrived = pl.pallas_call(
        in_order,
        out_shape=jax.ShapeDtypeStruct((images, both), BF16),
        in_specs=vmem(1),
        out_specs=vmem(1)[0],
        compiler_params=params(4),
        name="in_order",
    )(arrived)
    arrived = lax.all_gather(arrived, TOK, axis=0)

    leaving = pl.pallas_call(
        expert,
        out_shape=jax.ShapeDtypeStruct((quarters, images, both + 128), BF16),
        in_specs=[pl.BlockSpec(memory_space=pltpu.SMEM)] + vmem(3),
        out_specs=vmem(1)[0],
        compiler_params=params(12),
        name="expert",
    )(place, arrived, w_in[0], w_out[0])
    returned = exchanged(chip_sum(leaving, core))
    returned, totals = pl.pallas_call(
        in_order_with_totals,
        out_shape=(
            jax.ShapeDtypeStruct((slots, both), BF16),
            jax.ShapeDtypeStruct((8, slots), F32),
        ),
        in_specs=vmem(1),
        out_specs=vmem(2),
        compiler_params=params(4),
        name="in_order_with_totals",
    )(returned)
    returned = lax.all_gather(returned, TOK, axis=0)

    result = pl.pallas_call(
        tokens_back,
        out_shape=jax.ShapeDtypeStruct((rows, features), BF16),
        in_specs=vmem(7),
        out_specs=pl.BlockSpec(memory_space=pl.ANY),
        scratch_shapes=[VMEM((rows, features), BF16), pltpu.SemaphoreType.DMA((quarters,))],
        compiler_params=params(12),
        name="tokens_back",
    )(returned, totals, tokens, upstream, dispatch, combine, slot_keys)
    return result[None]


def solution(mesh):
    sizes = (2, 2, 4, 2, 16)
    fine = Mesh(mesh.devices.reshape(sizes), TOK + EXP)
    placed = (
        P(EXP, TOK, None),
        P(EXP, TOK, None),
        P(EXP, TOK, None),
        P(EXP, TOK, None),
        P(EXP, None, TOK),
        P(EXP, TOK, None),
        P(),
    )
    return jax.shard_map(
        body, mesh=fine, in_specs=placed, out_specs=P(EXP, TOK, None), check_vma=False
    )
```

```python
import jax
import jax.numpy as jnp
from jax import lax
from jax.experimental import pallas as pl
from jax.experimental.pallas import tpu as pltpu
from jax.sharding import Mesh
from jax.sharding import PartitionSpec as P

F32 = jnp.float32
BF16 = jnp.bfloat16
VMEM = pltpu.VMEM
MIB = 1024 * 1024


def dot(a, b, dims):
    return lax.dot_general(a, b, (dims, ((), ())), preferred_element_type=F32)


def opening(out_ref):
    out_ref[...] = jnp.zeros_like(out_ref)


def slot_sums(_, disp_ref, comb_ref, tok_ref, up_ref, out_ref):
    quarters, _, both = out_ref.shape
    width = both // 2
    for k, (weight, src) in enumerate(((disp_ref, tok_ref), (comb_ref, up_ref))):
        weight = weight[...].T
        for q in range(quarters):
            part = dot(weight, src[:, q * width : (q + 1) * width], ((1,), (0,)))
            out_ref[q, :, k * width : (k + 1) * width] = part.astype(BF16)


def gelu_parts(pre_act):
    inside = 0.7978845608 * (pre_act + 0.044715 * pre_act * pre_act * pre_act)
    tanh_val = jnp.tanh(inside)
    gelu_value = 0.5 * pre_act * (1.0 + tanh_val)
    gelu_slope = 0.5 * (1.0 + tanh_val) + 0.5 * pre_act * (
        1.0 - tanh_val * tanh_val
    ) * 0.7978845608 * (1.0 + 3.0 * 0.044715 * pre_act * pre_act)
    return gelu_value, gelu_slope


def expert(rows_ref, first_ref, second_ref, out_ref):
    quarters, _, both = rows_ref.shape
    width = both // 2
    inputs, grads = (
        jnp.concatenate([rows_ref[q, :, at : at + width] for q in range(quarters)], axis=1)
        for at in (0, width)
    )
    pre_act = dot(inputs, first_ref[...], ((1,), (0,)))
    hidden_grad = dot(grads, second_ref[...], ((1,), (1,)))
    value, slope = gelu_parts(pre_act)
    hidden = value.astype(BF16)
    pre_grad = (hidden_grad * slope).astype(BF16)
    for q in range(quarters):
        cols = slice(q * width, (q + 1) * width)
        out_ref[q, :, :width] = dot(hidden, second_ref[:, cols], ((1,), (0,))).astype(BF16)
        out_ref[q, :, width:] = dot(pre_grad, first_ref[cols, :], ((1,), (1,))).astype(BF16)


def transposed_rows(rows, inner):
    outer = rows // inner
    to = lax.broadcasted_iota(jnp.int32, (rows, rows), 0)
    at = lax.broadcasted_iota(jnp.int32, (rows, rows), 1)
    return (at == (to % outer) * inner + to // outer).astype(BF16)


def plane_sum(rows_ref, out_ref):
    rows = out_ref.shape[0]
    order = transposed_rows(rows, 16)
    total = dot(order, rows_ref[:rows, :], ((1,), (0,)))
    total += dot(order, rows_ref[rows:, :], ((1,), (0,)))
    out_ref[...] = total.astype(BF16)


def with_totals(back_ref, slots_ref, out_ref):
    rows, both = back_ref.shape
    width = both // 2
    order = transposed_rows(rows, rows // 16)
    back = dot(order, back_ref[...], ((1,), (0,)))
    out_ref[:rows, :] = back.astype(BF16)
    product = slots_ref[:, :width].astype(F32) * back[:, width:]
    high = product.astype(BF16)
    low = (product - high.astype(F32)).astype(BF16)
    ones = jnp.ones((16, width), BF16)
    total = dot(ones, high, ((1,), (1,))) + dot(ones, low, ((1,), (1,)))
    total_high = total.astype(BF16)
    out_ref[rows:, :rows] = total_high
    out_ref[rows:, rows : 2 * rows] = (total - total_high.astype(F32)).astype(BF16)
    out_ref[rows:, 2 * rows :] = jnp.zeros((16, both - 2 * rows), BF16)


def tokens_back(rows_ref, tok_ref, up_ref, disp_ref, comb_ref, keys_ref, out_hbm, out_ref, sems):
    quarters, _, both = rows_ref.shape
    slots = disp_ref.shape[1]
    width = both // 2
    comb_grad = disp_grad = totals = 0.0
    for q in range(quarters):
        cols = slice(q * width, (q + 1) * width)
        comb_grad += dot(up_ref[:, cols], rows_ref[q, :slots, :width], ((1,), (1,)))
        disp_grad += dot(tok_ref[:, cols], rows_ref[q, :slots, width:], ((1,), (1,)))
        totals += rows_ref[q, slots:, :slots].astype(F32)
        totals += rows_ref[q, slots:, slots : 2 * slots].astype(F32)
    comb = comb_ref[...].astype(F32)
    disp = disp_ref[...].astype(F32)
    logit = comb * (comb_grad - jnp.sum(comb * comb_grad, axis=1, keepdims=True))
    logit += disp * (disp_grad - totals[:1, :])
    logit = logit.astype(BF16)
    copies = []
    for q in range(quarters):
        cols = slice(q * width, (q + 1) * width)
        part = dot(disp_ref[...], rows_ref[q, :slots, width:], ((1,), (0,)))
        part += dot(logit, keys_ref[cols, :], ((1,), (1,)))
        out_ref[:, cols] = part.astype(BF16)
        block = pl.ds(q * width, width)
        copy = pltpu.make_async_copy(out_ref.at[:, block], out_hbm.at[:, block], sems.at[q])
        copy.start()
        copies.append(copy)
    for copy in copies:
        copy.wait()


def vmem(count):
    return [pl.BlockSpec(memory_space=VMEM)] * count


def params(mib):
    return pltpu.CompilerParams(vmem_limit_bytes=mib * MIB)


def pick(value, at, dim=0):
    return lax.dynamic_index_in_dim(value, at, dim, keepdims=False)


def core_terms(parts, core):
    given = pick(parts, 1 - core, 1)
    arrived = lax.all_gather(given, "core", axis=0)
    return pick(parts, core, 1), pick(arrived, 1 - core)


def tok_sum(parts, xl, core):
    terms = core_terms(parts, core)

    def half(at):
        return sum(pick(v, at).astype(F32) for v in terms)

    across = lax.all_gather(half(1 - xl).astype(BF16), "x_lo", axis=0)
    return half(xl) + pick(across, 1 - xl).astype(F32)


EXP = ("y", "x_hi", "z")
TOK = ("x_lo", "core")


def exchanged(value):
    rows, cols = value.shape
    blocks = value.reshape(rows, cols // 128, 128)
    return lax.all_to_all(blocks, EXP, split_axis=0, concat_axis=0, tiled=True).reshape(rows, cols)


def body(tokens, upstream, dispatch, combine, w_in, w_out, slot_keys):
    tokens, upstream, dispatch, combine = tokens[0], upstream[0], dispatch[0], combine[0]
    rows, features = tokens.shape
    slots = dispatch.shape[1]
    quarters = 4
    width = features // quarters
    both = 2 * width
    xl, core = lax.axis_index("x_lo"), lax.axis_index("core")
    parts = jax.ShapeDtypeStruct((quarters, slots, both), BF16)

    opened = pl.pallas_call(
        opening,
        out_shape=jax.ShapeDtypeStruct((8, 128), F32),
        out_specs=vmem(1)[0],
        compiler_params=params(1),
        cost_estimate=pl.CostEstimate(flops=10**10, bytes_accessed=10**7, transcendentals=0),
        name="opening",
    )()
    partial = pl.pallas_call(
        slot_sums,
        out_shape=parts,
        in_specs=vmem(5),
        out_specs=vmem(1)[0],
        compiler_params=params(8),
        name="slot_sums",
    )(opened, dispatch, combine, tokens, upstream)
    summed = tok_sum(partial.reshape(2, 2, slots, both), xl, core).astype(BF16)
    arrived = exchanged(summed)
    images = arrived.shape[0]
    arrived, w_in, w_out = lax.optimization_barrier((arrived, w_in, w_out))
    arrived = lax.all_gather(arrived, TOK, axis=0)

    leaving = pl.pallas_call(
        expert,
        out_shape=jax.ShapeDtypeStruct((quarters, images, both), BF16),
        in_specs=vmem(3),
        out_specs=vmem(1)[0],
        compiler_params=params(12),
        name="expert",
    )(arrived, w_in[0], w_out[0])
    terms = core_terms(leaving.reshape(2, 2, images, both), core)
    leaving = sum(v.astype(F32) for v in terms).astype(BF16)
    plane = ("x_lo", "y", "x_hi")
    leaving = lax.all_to_all(leaving.reshape(16, 16, both), plane, 0, 0, tiled=True)
    leaving = pl.pallas_call(
        plane_sum,
        out_shape=jax.ShapeDtypeStruct((slots, both), BF16),
        in_specs=vmem(1),
        out_specs=vmem(1)[0],
        compiler_params=params(4),
        name="plane_sum",
    )(leaving.reshape(2 * slots, both))
    leaving = leaving.reshape(16, slots // 16, both)
    returned = lax.all_to_all(leaving, "z", 0, 0, tiled=True).reshape(slots, both)
    returned = pl.pallas_call(
        with_totals,
        out_shape=jax.ShapeDtypeStruct((slots + 16, both), BF16),
        in_specs=vmem(2),
        out_specs=vmem(1)[0],
        compiler_params=params(4),
        name="with_totals",
    )(returned, summed)
    returned = lax.all_gather(returned, TOK, axis=0)

    result = pl.pallas_call(
        tokens_back,
        out_shape=jax.ShapeDtypeStruct((rows, features), BF16),
        in_specs=vmem(6),
        out_specs=pl.BlockSpec(memory_space=pl.ANY),
        scratch_shapes=[VMEM((rows, features), BF16), pltpu.SemaphoreType.DMA((quarters,))],
        compiler_params=params(12),
        name="tokens_back",
    )(returned, tokens, upstream, dispatch, combine, slot_keys)
    return result[None]


def solution(mesh):
    sizes = (2, 2, 4, 2, 16)
    fine = Mesh(mesh.devices.reshape(sizes), TOK + EXP)
    placed = (
        P(EXP, TOK, None),
        P(EXP, TOK, None),
        P(EXP, TOK, None),
        P(EXP, TOK, None),
        P(EXP, None, TOK),
        P(EXP, TOK, None),
        P(),
    )
    return jax.shard_map(
        body, mesh=fine, in_specs=placed, out_specs=P(EXP, TOK, None), check_vma=False
    )
```

```python
import jax
import jax.numpy as jnp
from jax import lax
from jax.experimental import pallas as pl
from jax.experimental.pallas import tpu as pltpu
from jax.sharding import Mesh
from jax.sharding import PartitionSpec as P

F32 = jnp.float32
BF16 = jnp.bfloat16
VMEM = pltpu.VMEM
MIB = 1024 * 1024


def dot(a, b, dims):
    return lax.dot_general(a, b, (dims, ((), ())), preferred_element_type=F32)


def opening(out_ref):
    out_ref[...] = jnp.zeros_like(out_ref)


def slot_sums(_, disp_ref, comb_ref, tok_ref, up_ref, out_ref):
    quarters, _, both = out_ref.shape
    width = both // 2
    for k, (weight, src) in enumerate(((disp_ref, tok_ref), (comb_ref, up_ref))):
        weight = weight[...].T
        for q in range(quarters):
            part = dot(weight, src[:, q * width : (q + 1) * width], ((1,), (0,)))
            out_ref[q, :, k * width : (k + 1) * width] = part.astype(BF16)


def gelu_parts(pre_act):
    inside = 0.7978845608 * (pre_act + 0.044715 * pre_act * pre_act * pre_act)
    tanh_val = jnp.tanh(inside)
    gelu_value = 0.5 * pre_act * (1.0 + tanh_val)
    gelu_slope = 0.5 * (1.0 + tanh_val) + 0.5 * pre_act * (
        1.0 - tanh_val * tanh_val
    ) * 0.7978845608 * (1.0 + 3.0 * 0.044715 * pre_act * pre_act)
    return gelu_value, gelu_slope


def expert(rows_ref, first_ref, second_ref, out_ref):
    quarters, _, both = rows_ref.shape
    width = both // 2
    inputs, grads = (
        jnp.concatenate([rows_ref[q, :, at : at + width] for q in range(quarters)], axis=1)
        for at in (0, width)
    )
    pre_act = dot(inputs, first_ref[...], ((1,), (0,)))
    hidden_grad = dot(grads, second_ref[...], ((1,), (1,)))
    value, slope = gelu_parts(pre_act)
    hidden = value.astype(BF16)
    pre_grad = (hidden_grad * slope).astype(BF16)
    for q in range(quarters):
        cols = slice(q * width, (q + 1) * width)
        out_ref[q, :, :width] = dot(hidden, second_ref[:, cols], ((1,), (0,))).astype(BF16)
        out_ref[q, :, width:] = dot(pre_grad, first_ref[cols, :], ((1,), (1,))).astype(BF16)


def transposed_rows(rows, inner):
    outer = rows // inner
    to = lax.broadcasted_iota(jnp.int32, (rows, rows), 0)
    at = lax.broadcasted_iota(jnp.int32, (rows, rows), 1)
    return (at == (to % outer) * inner + to // outer).astype(BF16)


def plane_sum(rows_ref, out_ref):
    rows = out_ref.shape[0]
    to = lax.broadcasted_iota(jnp.int32, (rows, 2 * rows), 0)
    at = lax.broadcasted_iota(jnp.int32, (rows, 2 * rows), 1)
    plane, z = at // 16 % 8, at % 16
    order = (to == z * 8 + plane).astype(BF16)
    out_ref[...] = dot(order, rows_ref[...], ((1,), (0,))).astype(BF16)


def with_totals(back_ref, slots_ref, out_ref):
    rows, both = back_ref.shape
    width = both // 2
    order = transposed_rows(rows, rows // 16)
    back = dot(order, back_ref[...], ((1,), (0,)))
    out_ref[:rows, :] = back.astype(BF16)
    product = slots_ref[:, :width].astype(F32) * back[:, width:]
    product = product[:, : width // 2] + product[:, width // 2 :]
    high = product.astype(BF16)
    low = (product - high.astype(F32)).astype(BF16)
    ones = jnp.ones((16, width // 2), BF16)
    total = dot(ones, high, ((1,), (1,))) + dot(ones, low, ((1,), (1,)))
    total_high = total.astype(BF16)
    out_ref[rows:, :rows] = total_high
    out_ref[rows:, rows : 2 * rows] = (total - total_high.astype(F32)).astype(BF16)
    out_ref[rows:, 2 * rows :] = jnp.zeros((16, both - 2 * rows), BF16)


def tokens_back(rows_ref, tok_ref, up_ref, disp_ref, comb_ref, keys_ref, out_hbm, out_ref, sems):
    quarters, _, both = rows_ref.shape
    slots = disp_ref.shape[1]
    width = both // 2
    comb_grad = disp_grad = totals = 0.0
    for q in range(quarters):
        cols = slice(q * width, (q + 1) * width)
        comb_grad += dot(up_ref[:, cols], rows_ref[q, :slots, :width], ((1,), (1,)))
        disp_grad += dot(tok_ref[:, cols], rows_ref[q, :slots, width:], ((1,), (1,)))
        totals += rows_ref[q, slots:, :slots].astype(F32)
        totals += rows_ref[q, slots:, slots : 2 * slots].astype(F32)
    comb = comb_ref[...].astype(F32)
    disp = disp_ref[...].astype(F32)
    logit = comb * (comb_grad - jnp.sum(comb * comb_grad, axis=1, keepdims=True))
    logit += disp * (disp_grad - totals[:1, :])
    logit = logit.astype(BF16)
    copies = []
    for q in range(quarters):
        cols = slice(q * width, (q + 1) * width)
        part = dot(disp_ref[...], rows_ref[q, :slots, width:], ((1,), (0,)))
        part += dot(logit, keys_ref[cols, :], ((1,), (1,)))
        out_ref[:, cols] = part.astype(BF16)
        block = pl.ds(q * width, width)
        copy = pltpu.make_async_copy(out_ref.at[:, block], out_hbm.at[:, block], sems.at[q])
        copy.start()
        copies.append(copy)
    for copy in copies:
        copy.wait()


def vmem(count):
    return [pl.BlockSpec(memory_space=VMEM)] * count


def params(mib):
    return pltpu.CompilerParams(vmem_limit_bytes=mib * MIB)


def pick(value, at, dim=0):
    return lax.dynamic_index_in_dim(value, at, dim, keepdims=False)


def core_terms(parts, core):
    given = pick(parts, 1 - core, 1)
    arrived = lax.all_gather(given, "core", axis=0)
    return pick(parts, core, 1), pick(arrived, 1 - core)


def tok_sum(parts, xl, core):
    terms = core_terms(parts, core)

    def half(at):
        return sum(pick(v, at).astype(F32) for v in terms)

    across = lax.all_gather(half(1 - xl).astype(BF16), "x_lo", axis=0)
    return half(xl) + pick(across, 1 - xl).astype(F32)


EXP = ("y", "x_hi", "z")
TOK = ("x_lo", "core")


def exchanged(value):
    rows, cols = value.shape
    blocks = value.reshape(rows, cols // 128, 128)
    return lax.all_to_all(blocks, EXP, split_axis=0, concat_axis=0, tiled=True).reshape(rows, cols)


def body(tokens, upstream, dispatch, combine, w_in, w_out, slot_keys):
    tokens, upstream, dispatch, combine = tokens[0], upstream[0], dispatch[0], combine[0]
    rows, features = tokens.shape
    slots = dispatch.shape[1]
    quarters = 4
    width = features // quarters
    both = 2 * width
    xl, core = lax.axis_index("x_lo"), lax.axis_index("core")
    parts = jax.ShapeDtypeStruct((quarters, slots, both), BF16)

    opened = pl.pallas_call(
        opening,
        out_shape=jax.ShapeDtypeStruct((8, 128), F32),
        out_specs=vmem(1)[0],
        compiler_params=params(1),
        cost_estimate=pl.CostEstimate(flops=10**10, bytes_accessed=10**7, transcendentals=0),
        name="opening",
    )()
    partial = pl.pallas_call(
        slot_sums,
        out_shape=parts,
        in_specs=vmem(5),
        out_specs=vmem(1)[0],
        compiler_params=params(8),
        name="slot_sums",
    )(opened, dispatch, combine, tokens, upstream)
    summed = tok_sum(partial.reshape(2, 2, slots, both), xl, core).astype(BF16)
    arrived = exchanged(summed)
    images = arrived.shape[0]
    arrived, w_in, w_out = lax.optimization_barrier((arrived, w_in, w_out))
    arrived = lax.all_gather(arrived, TOK, axis=0)

    leaving = pl.pallas_call(
        expert,
        out_shape=jax.ShapeDtypeStruct((quarters, images, both), BF16),
        in_specs=vmem(3),
        out_specs=vmem(1)[0],
        compiler_params=params(12),
        name="expert",
    )(arrived, w_in[0], w_out[0])
    terms = core_terms(leaving.reshape(2, 2, images, both), core)
    leaving = sum(v.astype(F32) for v in terms).astype(BF16)
    plane = ("x_lo", "y", "x_hi")
    leaving = lax.all_to_all(leaving.reshape(16, 16, both), plane, 0, 0, tiled=True)
    leaving = pl.pallas_call(
        plane_sum,
        out_shape=jax.ShapeDtypeStruct((slots, both), BF16),
        in_specs=vmem(1),
        out_specs=vmem(1)[0],
        compiler_params=params(4),
        name="plane_sum",
    )(leaving.reshape(2 * slots, both))
    leaving = leaving.reshape(16, slots // 16, both)
    returned = lax.all_to_all(leaving, "z", 0, 0, tiled=True).reshape(slots, both)
    returned = pl.pallas_call(
        with_totals,
        out_shape=jax.ShapeDtypeStruct((slots + 16, both), BF16),
        in_specs=vmem(2),
        out_specs=vmem(1)[0],
        compiler_params=params(4),
        name="with_totals",
    )(returned, summed)
    returned = lax.all_gather(returned, TOK, axis=0)

    result = pl.pallas_call(
        tokens_back,
        out_shape=jax.ShapeDtypeStruct((rows, features), BF16),
        in_specs=vmem(6),
        out_specs=pl.BlockSpec(memory_space=pl.ANY),
        scratch_shapes=[VMEM((rows, features), BF16), pltpu.SemaphoreType.DMA((quarters,))],
        compiler_params=params(12),
        name="tokens_back",
    )(returned, tokens, upstream, dispatch, combine, slot_keys)
    return result[None]


def solution(mesh):
    sizes = (2, 2, 4, 2, 16)
    fine = Mesh(mesh.devices.reshape(sizes), TOK + EXP)
    placed = (
        P(EXP, TOK, None),
        P(EXP, TOK, None),
        P(EXP, TOK, None),
        P(EXP, TOK, None),
        P(EXP, None, TOK),
        P(EXP, TOK, None),
        P(),
    )
    return jax.shard_map(
        body, mesh=fine, in_specs=placed, out_specs=P(EXP, TOK, None), check_vma=False
    )
```

```python
import jax
import jax.numpy as jnp
from jax import lax
from jax.experimental import pallas as pl
from jax.experimental.pallas import tpu as pltpu
from jax.sharding import Mesh
from jax.sharding import PartitionSpec as P

F32 = jnp.float32
BF16 = jnp.bfloat16
VMEM = pltpu.VMEM
MIB = 1024 * 1024


def dot(a, b, dims):
    return lax.dot_general(a, b, (dims, ((), ())), preferred_element_type=F32)


def opening(out_ref):
    out_ref[...] = jnp.zeros_like(out_ref)


def slot_sums(_, disp_ref, comb_ref, tok_ref, up_ref, out_ref):
    quarters, _, both = out_ref.shape
    width = both // 2
    for k, (weight, src) in enumerate(((disp_ref, tok_ref), (comb_ref, up_ref))):
        weight = weight[...].T
        for q in range(quarters):
            part = dot(weight, src[:, q * width : (q + 1) * width], ((1,), (0,)))
            out_ref[q, :, k * width : (k + 1) * width] = part.astype(BF16)


def gelu_parts(pre_act):
    inside = 0.7978845608 * (pre_act + 0.044715 * pre_act * pre_act * pre_act)
    tanh_val = jnp.tanh(inside)
    gelu_value = 0.5 * pre_act * (1.0 + tanh_val)
    gelu_slope = 0.5 * (1.0 + tanh_val) + 0.5 * pre_act * (
        1.0 - tanh_val * tanh_val
    ) * 0.7978845608 * (1.0 + 3.0 * 0.044715 * pre_act * pre_act)
    return gelu_value, gelu_slope


def expert(rows_ref, first_ref, second_ref, out_ref):
    quarters, _, both = rows_ref.shape
    width = both // 2
    inputs, grads = (
        jnp.concatenate([rows_ref[q, :, at : at + width] for q in range(quarters)], axis=1)
        for at in (0, width)
    )
    pre_act = dot(inputs, first_ref[...], ((1,), (0,)))
    hidden_grad = dot(grads, second_ref[...], ((1,), (1,)))
    value, slope = gelu_parts(pre_act)
    hidden = value.astype(BF16)
    pre_grad = (hidden_grad * slope).astype(BF16)
    for q in range(quarters):
        cols = slice(q * width, (q + 1) * width)
        out_ref[q, :, :width] = dot(hidden, second_ref[:, cols], ((1,), (0,))).astype(BF16)
        out_ref[q, :, width:] = dot(pre_grad, first_ref[cols, :], ((1,), (1,))).astype(BF16)


def transposed_rows(rows, inner):
    outer = rows // inner
    to = lax.broadcasted_iota(jnp.int32, (rows, rows), 0)
    at = lax.broadcasted_iota(jnp.int32, (rows, rows), 1)
    return (at == (to % outer) * inner + to // outer).astype(BF16)


def plane_sum(rows_ref, out_ref):
    rows = out_ref.shape[0]
    to = lax.broadcasted_iota(jnp.int32, (rows, 2 * rows), 0)
    at = lax.broadcasted_iota(jnp.int32, (rows, 2 * rows), 1)
    plane, z = at // 16 % 8, at % 16
    order = (to == z * 8 + plane).astype(BF16)
    out_ref[...] = dot(order, rows_ref[...], ((1,), (0,))).astype(BF16)


def with_totals(back_ref, slots_ref, out_ref):
    rows, both = back_ref.shape
    width = both // 2
    order = transposed_rows(rows, rows // 16)
    back = dot(order, back_ref[...], ((1,), (0,)))
    out_ref[:rows, :] = back.astype(BF16)
    product = slots_ref[:, :width].astype(F32) * back[:, width:]
    product = product[:, : width // 2] + product[:, width // 2 :]
    high = product.astype(BF16)
    low = (product - high.astype(F32)).astype(BF16)
    ones = jnp.ones((16, width // 2), BF16)
    total = dot(ones, high, ((1,), (1,))) + dot(ones, low, ((1,), (1,)))
    total_high = total.astype(BF16)
    out_ref[rows:, :rows] = total_high
    out_ref[rows:, rows : 2 * rows] = (total - total_high.astype(F32)).astype(BF16)
    out_ref[rows:, 2 * rows :] = jnp.zeros((16, both - 2 * rows), BF16)


def tokens_back(rows_ref, tok_ref, up_ref, disp_ref, comb_ref, keys_ref, out_hbm, out_ref, sems):
    quarters, _, both = rows_ref.shape
    slots = disp_ref.shape[1]
    width = both // 2
    comb_grad = disp_grad = totals = 0.0
    for q in range(quarters):
        cols = slice(q * width, (q + 1) * width)
        comb_grad += dot(up_ref[:, cols], rows_ref[q, :slots, :width], ((1,), (1,)))
        disp_grad += dot(tok_ref[:, cols], rows_ref[q, :slots, width:], ((1,), (1,)))
        totals += rows_ref[q, slots:, :slots].astype(F32)
        totals += rows_ref[q, slots:, slots : 2 * slots].astype(F32)
    comb = comb_ref[...].astype(F32)
    disp = disp_ref[...].astype(F32)
    logit = comb * (comb_grad - jnp.sum(comb * comb_grad, axis=1, keepdims=True))
    logit += disp * (disp_grad - totals[:1, :])
    logit = logit.astype(BF16)
    copies = []
    for q in range(quarters):
        cols = slice(q * width, (q + 1) * width)
        part = dot(disp_ref[...], rows_ref[q, :slots, width:], ((1,), (0,)))
        part += dot(logit, keys_ref[cols, :], ((1,), (1,)))
        out_ref[:, cols] = part.astype(BF16)
        block = pl.ds(q * width, width)
        copy = pltpu.make_async_copy(out_ref.at[:, block], out_hbm.at[:, block], sems.at[q])
        copy.start()
        copies.append(copy)
    for copy in copies:
        copy.wait()


def vmem(count):
    return [pl.BlockSpec(memory_space=VMEM)] * count


def params(mib):
    return pltpu.CompilerParams(vmem_limit_bytes=mib * MIB)


def pick(value, at, dim=0):
    return lax.dynamic_index_in_dim(value, at, dim, keepdims=False)


def core_terms(parts, core):
    given = pick(parts, 1 - core, 1)
    arrived = lax.all_gather(given, "core", axis=0)
    return pick(parts, core, 1), pick(arrived, 1 - core)


def tok_sum(parts, xl, core):
    terms = core_terms(parts, core)

    def half(at):
        return sum(pick(v, at).astype(F32) for v in terms)

    across = lax.all_gather(half(1 - xl).astype(BF16), "x_lo", axis=0)
    return half(xl) + pick(across, 1 - xl).astype(F32)


EXP = ("y", "x_hi", "z")
TOK = ("x_lo", "core")


def exchanged(value):
    rows, cols = value.shape
    blocks = value.reshape(rows, cols // 128, 128)
    return lax.all_to_all(blocks, EXP, split_axis=0, concat_axis=0, tiled=True).reshape(rows, cols)


def body(tokens, upstream, dispatch, combine, w_in, w_out, slot_keys):
    tokens, upstream, dispatch, combine = tokens[0], upstream[0], dispatch[0], combine[0]
    rows, features = tokens.shape
    slots = dispatch.shape[1]
    quarters = 4
    width = features // quarters
    both = 2 * width
    xl, core = (lax.axis_index(axis).astype(jnp.uint32) for axis in TOK)
    parts = jax.ShapeDtypeStruct((quarters, slots, both), BF16)

    opened = pl.pallas_call(
        opening,
        out_shape=jax.ShapeDtypeStruct((8, 128), F32),
        out_specs=vmem(1)[0],
        compiler_params=params(1),
        cost_estimate=pl.CostEstimate(flops=10**10, bytes_accessed=10**7, transcendentals=0),
        name="opening",
    )()
    partial = pl.pallas_call(
        slot_sums,
        out_shape=parts,
        in_specs=vmem(5),
        out_specs=vmem(1)[0],
        compiler_params=params(8),
        name="slot_sums",
    )(opened, dispatch, combine, tokens, upstream)
    summed = tok_sum(partial.reshape(2, 2, slots, both), xl, core).astype(BF16)
    arrived = exchanged(summed)
    images = arrived.shape[0]
    arrived, w_in, w_out = lax.optimization_barrier((arrived, w_in, w_out))
    arrived = lax.all_gather(arrived, TOK, axis=0)

    leaving = pl.pallas_call(
        expert,
        out_shape=jax.ShapeDtypeStruct((quarters, images, both), BF16),
        in_specs=vmem(3),
        out_specs=vmem(1)[0],
        compiler_params=params(12),
        name="expert",
    )(arrived, w_in[0], w_out[0])
    terms = core_terms(leaving.reshape(2, 2, images, both), core)
    leaving = sum(v.astype(F32) for v in terms).astype(BF16)
    plane = ("x_lo", "y", "x_hi")
    leaving = lax.all_to_all(leaving.reshape(16, 16, both), plane, 0, 0, tiled=True)
    leaving = pl.pallas_call(
        plane_sum,
        out_shape=jax.ShapeDtypeStruct((slots, both), BF16),
        in_specs=vmem(1),
        out_specs=vmem(1)[0],
        compiler_params=params(4),
        name="plane_sum",
    )(leaving.reshape(2 * slots, both))
    leaving = leaving.reshape(16, slots // 16, both)
    returned = lax.all_to_all(leaving, "z", 0, 0, tiled=True).reshape(slots, both)
    returned = pl.pallas_call(
        with_totals,
        out_shape=jax.ShapeDtypeStruct((slots + 16, both), BF16),
        in_specs=vmem(2),
        out_specs=vmem(1)[0],
        compiler_params=params(4),
        name="with_totals",
    )(returned, summed)
    returned = lax.all_gather(returned, TOK, axis=0)

    result = pl.pallas_call(
        tokens_back,
        out_shape=jax.ShapeDtypeStruct((rows, features), BF16),
        in_specs=vmem(6),
        out_specs=pl.BlockSpec(memory_space=pl.ANY),
        scratch_shapes=[VMEM((rows, features), BF16), pltpu.SemaphoreType.DMA((quarters,))],
        compiler_params=params(12),
        name="tokens_back",
    )(returned, tokens, upstream, dispatch, combine, slot_keys)
    return result[None]


def solution(mesh):
    sizes = (2, 2, 4, 2, 16)
    fine = Mesh(mesh.devices.reshape(sizes), TOK + EXP)
    placed = (
        P(EXP, TOK, None),
        P(EXP, TOK, None),
        P(EXP, TOK, None),
        P(EXP, TOK, None),
        P(EXP, None, TOK),
        P(EXP, TOK, None),
        P(),
    )
    return jax.shard_map(
        body, mesh=fine, in_specs=placed, out_specs=P(EXP, TOK, None), check_vma=False
    )
```
